256 devices in a mesh: blk: 8 (over z_lo, x), head: 32 (over y, z_hi, core).
Axes of the slice: x: 4, y: 4, z: 8 (z_hi: 4, z_lo: 2; z = z_hi * 2 + z_lo), core: 2. Of those that a mesh axis runs over, the one named last changes fastest.
Arguments:
- query_rows: bfloat16 [32768, 4096], P(('blk', 'head')), may hold values from -12 to 12
- key_rows: bfloat16 [32768, 4096], P(('blk', 'head')), may hold values from -12 to 12
- value_rows: bfloat16 [32768, 4096], P(('blk', 'head')), may hold values from -6 to 6
- block_lists: int32 [32, 256, 16], P('head', 'blk'), may hold values from 0 to 255, as said below
Outputs:
- mixed: bfloat16 [32768, 4096], P(('blk', 'head'))
The draws below stay inside these ranges and needn't reach their ends.
Inputs may be any that keep to these rules, and one draw needn't show every extreme that they name: Each row block_lists[h, i, :] names 16 distinct key blocks in ascending order; they may lie anywhere in the clip.
All inputs are finite; a program needn't handle non-finite values.
Results may differ from the reference program's by a relative error of at most 0.007.
Values may be sent and summed in bfloat16 or wider, within the bound.
A program may use at most 128 MiB of HBM per device.

```python
import jax
import jax.numpy as jnp
from jax import lax

HEADS = 32
HDIM = 128
BLOCK = 128
LIVE = 16
D = 4096
TOKENS = 32768


def draw_query_rows(key, part):
    key = jax.random.fold_in(key, 3)
    second_key = jax.random.fold_in(key, 1)
    return jnp.clip(jax.random.normal(second_key, (TOKENS, D), jnp.float32), -6.0, 6.0).astype(jnp.bfloat16)


def draw_key_rows(key, part):
    key = jax.random.fold_in(key, 5)
    second_key = jax.random.fold_in(key, 1)
    return jnp.clip(jax.random.normal(second_key, (TOKENS, D), jnp.float32), -6.0, 6.0).astype(jnp.bfloat16)


def draw_block_lists(key, part):
    key = jax.random.fold_in(key, 11)
    kind_key, jitter_key, phase_key, far_key, other_key = jax.random.split(key, 5)
    block_total = TOKENS // BLOCK
    stride = block_total // LIVE
    window_len = LIVE - 2
    outside = block_total - window_len
    pattern = jax.random.randint(kind_key, (HEADS, 1, 1), 0, 2)
    query_block = jnp.arange(block_total, dtype=jnp.int32)[None, :, None]
    window_column = jnp.arange(window_len, dtype=jnp.int32)[None, None, :]
    column = jnp.arange(LIVE, dtype=jnp.int32)[None, None, :]
    jitter = jax.random.randint(jitter_key, (HEADS, block_total, 1), -2, 3)
    window_start = jnp.clip(query_block - window_len // 2 + jitter, 0, block_total - window_len)
    window = jnp.broadcast_to(window_start + window_column, (HEADS, block_total, window_len))
    first_far = jax.random.randint(far_key, (HEADS, block_total, 1), 0, outside)
    second_far = jax.random.randint(other_key, (HEADS, block_total, 1), 0, outside - 1)
    second_far = second_far + (second_far >= first_far).astype(jnp.int32)
    far_blocks = jnp.concatenate([first_far, second_far], axis=2)
    far_blocks = far_blocks + (far_blocks >= window_start).astype(jnp.int32) * window_len
    spatial = jnp.sort(jnp.concatenate([window, far_blocks], axis=2), axis=2)
    phase = jax.random.randint(phase_key, (HEADS, 1, 1), 0, stride)
    temporal = (query_block + phase) % stride + column * stride
    return jnp.where(pattern == 0, spatial, temporal).astype(jnp.int32)


def level_of(key, shape, cuts, least, top_value):
    level, own = 1.0, jax.random.fold_in(key, 6)
    for dim, parts in cuts:
        draws = jnp.exp(jax.random.uniform(jax.random.fold_in(own, dim), (parts,), jnp.float32, least / len(cuts), top_value / len(cuts)))
        level = level * jnp.repeat(draws, shape[dim] // parts).reshape([-1 if axis == dim else 1 for axis in range(len(shape))])
    return level


def bell_draw(own_key, shape, spread, limit, cuts=(), kind=jnp.bfloat16):
    array = jax.random.normal(own_key, shape, jnp.float32) * spread
    if len(cuts) > 0:
        array = level_of(own_key, shape, cuts, -0.22, 0.18) * array
    return jnp.clip(array, min=-limit, max=limit).astype(kind)


def setup_inputs(seed: int = 0) -> dict:
    seeds = jax.random.split(jax.random.key(seed), 5)
    return {
        "query_rows": draw_query_rows(jax.random.fold_in(seeds[4], 71), 0),
        "key_rows": draw_key_rows(jax.random.fold_in(seeds[4], 71), 0),
        "value_rows": bell_draw(seeds[2], (TOKENS, D), 1.0, 6.0, ((0, 256),)),
        "block_lists": draw_block_lists(jax.random.fold_in(seeds[4], 71), 0),
    }


def reference(query_rows, key_rows, value_rows, block_lists):
    score_scale = HDIM ** -0.5
    seq_len = query_rows.shape[0]
    block_total = seq_len // BLOCK

    def split_heads(rows):
        return rows.reshape(block_total, BLOCK, HEADS, HDIM).transpose(2, 0, 1, 3)

    queries = split_heads(query_rows)
    keyset = split_heads(key_rows)
    valueset = split_heads(value_rows)

    def one_head(inputs):
        head_query, head_keys, head_values, head_lists = inputs

        def one_block(pair):
            block_query, entries = pair
            picked_keys = head_keys[entries].reshape(LIVE * BLOCK, HDIM)
            picked_values = head_values[entries].reshape(LIVE * BLOCK, HDIM)
            scores = jnp.dot(block_query, picked_keys.T, preferred_element_type=jnp.float32) * score_scale
            peak_value = jnp.max(scores, axis=1, keepdims=True)
            raw_weights = jnp.exp(scores - peak_value)
            total_sum = jnp.sum(raw_weights, axis=1, keepdims=True)
            blended = jnp.dot(raw_weights.astype(jnp.bfloat16), picked_values, preferred_element_type=jnp.float32)
            return (blended / total_sum).astype(jnp.bfloat16)

        return lax.map(one_block, (head_query, head_lists))

    result = lax.map(one_head, (queries, keyset, valueset, block_lists))
    return result.transpose(1, 2, 0, 3).reshape(seq_len, HEADS * HDIM)
```

```python
import math

import jax
import jax.numpy as jnp
from jax import lax
from jax.experimental import pallas as pl
from jax.experimental.pallas import tpu as pltpu
from jax.sharding import PartitionSpec as P

MESH = pl.DeviceIdType.MESH
BLOCK = 128
LIVE = 16
NX, NY, NZ = 4, 4, 8
EXP_SCALE = (128**-0.5) * math.log2(math.e)


def device(x, y, z, c):
    return ((z % 2) * NX + x, (y * (NZ // 2) + z // 2) * 2 + c)


def dz_of(g):
    return jnp.where(g % 2 == 1, (g + 1) // 2, (NZ - g // 2) % NZ)


def remote(src, dst, send_sem, recv_sem, to):
    copy = pltpu.make_async_remote_copy(
        src_ref=src, dst_ref=dst, send_sem=send_sem, recv_sem=recv_sem, device_id=to, device_id_type=MESH
    )
    copy.start()


def attend(q, ks, vs):
    s = lax.dot_general(q, jnp.concatenate(ks, axis=0), (((1,), (1,)), ((), ())), preferred_element_type=jnp.float32)
    m = jnp.max(s, axis=1, keepdims=True)
    p = jnp.exp2((s - m) * EXP_SCALE)
    total = jnp.sum(p, axis=1, keepdims=True)
    o = lax.dot_general(
        p.astype(jnp.bfloat16), jnp.concatenate(vs, axis=0), (((1,), (0,)), ((), ())), preferred_element_type=jnp.float32
    )
    return (o / total).astype(jnp.bfloat16)


def kernel(
    q_hbm, k_hbm, v_hbm, lists_hbm, out_hbm,
    kv, qbuf, obuf, lists_v, slots_v, slots,
    a_send, a_recv, x_send, left_recv, right_recv, far_recv, c_send, c_recv,
    l_send, l_recv, s_sem, o_send, o_recv,
):
    blk, head = lax.axis_index("blk"), lax.axis_index("head")
    x, z_lo = blk % NX, blk // NX
    y, z_hi, c = head // NZ, (head // 2) % (NZ // 2), head % 2
    z = z_hi * 2 + z_lo
    right, left = device((x + 1) % NX, y, z, c), device((x + NX - 1) % NX, y, z, c)
    other = device(x, y, z, 1 - c)
    my_head = y * NZ + z

    def slab(xx, zz):
        return ((c * NX + xx) * NZ + zz) * NY

    barrier = pltpu.get_barrier_semaphore()

    def greet(to):
        pl.semaphore_signal(barrier, inc=1, device_id=to, device_id_type=MESH)

    for dy in range(NY):
        for dz in range(NZ):
            if dy or dz:
                greet(device(x, (y + dy) % NY, (z + dz) % NZ, c))
    greet(right)
    greet(left)
    greet(other)
    greet(device(x, y, z + 1 - 2 * z_lo, 1 - c))
    pl.semaphore_wait(barrier, NY * NZ - 1 + 4)

    owner_z = z_hi * 2 + c
    remote(lists_hbm.at[0], lists_v.at[z_lo], l_send, l_recv, device(x, y, owner_z, 1 - c))

    @pl.when(z_lo == c)
    def _():
        pltpu.make_async_copy(lists_hbm.at[0], lists_v.at[z_lo], l_recv).start()

    @pl.when(z_lo != c)
    def _():
        remote(lists_hbm.at[0], lists_v.at[z_lo], l_send, l_recv, device(x, y, owner_z, c))

    for t, rows in enumerate((k_hbm, v_hbm, q_hbm)):

        def target(zz, yy, t=t):
            return qbuf.at[zz * NY + yy] if t == 2 else kv.at[t, slab(x, zz) + yy]

        def piece(zz, yy, rows=rows):
            return rows.at[:, pl.ds(pl.multiple_of((yy * NZ + zz) * BLOCK, BLOCK), BLOCK)]

        pltpu.make_async_copy(piece(z, y), target(z, y), a_recv.at[t, 0]).start()
        for dy in range(1, NY):
            yy = (y + dy) % NY
            remote(piece(z, yy), target(z, y), a_send.at[t], a_recv.at[t, 0], device(x, yy, z, c))

        def send(g, _, t=t, piece=piece, target=target):
            zz = (z + dz_of(g)) % NZ
            for dy in range(NY):
                yy = (y + dy) % NY
                remote(piece(zz, yy), target(z, y), a_send.at[t], a_recv.at[t, g], device(x, yy, zz, c))
            return 0

        lax.fori_loop(1, NZ, send, 0)

    steps = 2 * NZ

    def wait(ref, sem):
        pltpu.make_async_copy(ref, ref, sem).wait()

    def gather(s, _):
        @pl.when(s < steps)
        def _():
            t, g = s // NZ, s % NZ
            zz = (z + NZ - dz_of(g)) % NZ
            own = kv.at[t, pl.ds(slab(x, zz), NY)]
            wait(own, a_recv.at[t, g])
            remote(own, own, x_send.at[0], left_recv.at[t, g], right)
            remote(own, own, x_send.at[1], right_recv.at[t, g], left)
            remote(own, own, c_send, c_recv, other)

        @pl.when((s >= 2) & (s < steps + 2))
        def _():
            t, g = (s - 2) // NZ, (s - 2) % NZ
            zz = (z + NZ - dz_of(g)) % NZ
            base = slab((x + NX - 1) % NX, zz)
            chunk = kv.at[t, pl.ds(base, NY)]
            half = kv.at[t, pl.ds(base, NY // 2)]
            wait(chunk, left_recv.at[t, g])
            remote(half, half, x_send.at[2], far_recv.at[t, g], right)
            remote(chunk, chunk, c_send, c_recv, other)
            base = slab((x + 1) % NX, zz)
            chunk = kv.at[t, pl.ds(base, NY)]
            half = kv.at[t, pl.ds(base + NY // 2, NY // 2)]
            wait(chunk, right_recv.at[t, g])
            remote(half, half, x_send.at[2], far_recv.at[t, g], left)
            remote(chunk, chunk, c_send, c_recv, other)

        @pl.when(s >= 4)
        def _():
            t, g = (s - 4) // NZ, (s - 4) % NZ
            zz = (z + NZ - dz_of(g)) % NZ
            chunk = kv.at[t, pl.ds(slab((x + 2) % NX, zz), NY)]
            wait(chunk, far_recv.at[t, g])
            remote(chunk, chunk, c_send, c_recv, other)

        return 0

    lax.fori_loop(0, steps + 4, gather, 0)

    wait(lists_v, l_recv)
    i = lists_v[...]
    slots_v[...] = (((i & 1) * NX + ((i >> 5) & 3)) * NZ + ((i >> 1) & 3) * 2 + (i >> 7)) * NY + ((i >> 3) & 3)
    to_smem = pltpu.make_async_copy(slots_v, slots, s_sem)
    to_smem.start()
    to_smem.wait()

    for g in range(NZ):
        zz = (z + NZ - dz_of(g)) % NZ
        wait(qbuf.at[pl.ds(zz * NY, NY)], a_recv.at[2, g])
    wait(kv.at[:, pl.ds((1 - c) * NX * NZ * NY, NX * NZ * NY)], c_recv)

    def one_block(dy, dz):
        yy, zz = (y + dy) % NY, (z + dz) % NZ
        row = (yy * (NZ // 2) + zz // 2) * 2 + c
        places = [slots[zz % 2, row, j] for j in range(LIVE)]
        n = zz * NY + yy
        obuf[n] = attend(qbuf[n], [kv[0, p] for p in places], [kv[1, p] for p in places])
        mine = out_hbm.at[:, pl.ds(pl.multiple_of(my_head * BLOCK, BLOCK), BLOCK)]
        return obuf.at[n], mine, device(x, yy, zz, c)

    def pair(p, _):
        near, r = p - 14, p - 2
        dz_a = jnp.where(p < 2, 4, jnp.where(p < 14, 3 - r // 4, 0))
        dz_b = (NZ - dz_a) % NZ
        dy_a = jnp.where(p < 2, 2 * p, jnp.where(p < 14, (r + NY) % NY, 1 + near))
        dy_b = jnp.where(p < 2, 2 * p + 1, jnp.where(p < 14, (r + NY) % NY, (3 - 3 * near + NY) % NY))
        src_a, mine, to_a = one_block(dy_a, dz_a)
        remote(src_a, mine, o_send, o_recv, to_a)
        src_b, mine, to_b = one_block(dy_b, dz_b)

        @pl.when(p < 15)
        def _():
            remote(src_b, mine, o_send, o_recv, to_b)

        @pl.when(p == 15)
        def _():
            pltpu.make_async_copy(src_b, mine, o_recv).start()

        return 0

    lax.fori_loop(0, 16, pair, 0)

    for t in range(3):
        wait(kv.at[0, pl.ds(0, NY * NZ - 1)], a_send.at[t])
    for i in range(3):
        wait(kv.at[:, pl.ds(0, NZ * NY)], x_send.at[i])
    wait(kv.at[:, pl.ds(c * NX * NZ * NY, NX * NZ * NY)], c_send)
    wait(lists_v.at[0], l_send)

    @pl.when(z_lo != c)
    def _():
        wait(lists_v.at[0], l_send)

    wait(obuf.at[pl.ds(0, NY * NZ - 1)], o_send)
    wait(out_hbm, o_recv)


def on_device(query_rows, key_rows, value_rows, block_lists):
    dma = pltpu.SemaphoreType.DMA
    return pl.pallas_call(
        kernel,
        out_shape=jax.ShapeDtypeStruct(query_rows.shape, jnp.bfloat16),
        in_specs=[pl.BlockSpec(memory_space=pl.ANY)] * 4,
        out_specs=pl.BlockSpec(memory_space=pl.ANY),
        scratch_shapes=[
            pltpu.VMEM((2, 256, BLOCK, BLOCK), jnp.bfloat16),
            pltpu.VMEM((NY * NZ, BLOCK, BLOCK), jnp.bfloat16),
            pltpu.VMEM((NY * NZ, BLOCK, BLOCK), jnp.bfloat16),
            pltpu.VMEM((2, 32, LIVE), jnp.int32),
            pltpu.VMEM((2, 32, LIVE), jnp.int32),
            pltpu.SMEM((2, 32, LIVE), jnp.int32),
            dma((3,)), dma((3, NZ)), dma((3,)), dma((2, NZ)), dma((2, NZ)), dma((2, NZ)), dma, dma,
            dma, dma, dma, dma, dma,
        ],
        compiler_params=pltpu.CompilerParams(collective_id=0, has_side_effects=True, vmem_limit_bytes=48 * 2**20),
        name="attention",
    )(query_rows, key_rows, value_rows, block_lists)


def solution(mesh):
    in_specs = (P(("blk", "head"), None), P(("blk", "head"), None), P(("blk", "head"), None), P("head", "blk", None))
    return jax.shard_map(
        on_device, mesh=mesh, in_specs=in_specs, out_specs=P(("blk", "head"), None), check_vma=False
    )
```

```python
import math

import jax
import jax.numpy as jnp
from jax import lax
from jax.experimental import pallas as pl
from jax.experimental.pallas import tpu as pltpu
from jax.sharding import PartitionSpec as P

MESH = pl.DeviceIdType.MESH
BLOCK = 128
LIVE = 16
NX, NY, NZ = 4, 4, 8
HALF = NX * NY * NZ
EXP_SCALE = (128**-0.5) * math.log2(math.e)


def device(x, y, z, c):
    return ((z % 2) * NX + x, (y * (NZ // 2) + z // 2) * 2 + c)


def dz_of(g):
    return jnp.where(g % 2 == 1, (g + 1) // 2, (NZ - g // 2) % NZ)


def remote(src, dst, send_sem, recv_sem, to):
    copy = pltpu.make_async_remote_copy(
        src_ref=src, dst_ref=dst, send_sem=send_sem, recv_sem=recv_sem, device_id=to, device_id_type=MESH
    )
    copy.start()


def wait(ref, sem):
    pltpu.make_async_copy(ref, ref, sem).wait()


def kernel(
    q_hbm, k_hbm, v_hbm, lists_hbm, out_hbm,
    kbuf, vbuf, qbuf, obuf, weights, totals, lists_v, slots_v, slots,
    a_send, near_recv, a_recv, x_send, left_recv, right_recv, far_recv, c_send, c_recv,
    l_send, l_recv, s_sem, o_send, o_recv,
):
    blk, head = lax.axis_index("blk"), lax.axis_index("head")
    x, z_lo = blk % NX, blk // NX
    y, z_hi, c = head // NZ, (head // 2) % (NZ // 2), head % 2
    z = z_hi * 2 + z_lo
    right, left = device((x + 1) % NX, y, z, c), device((x + NX - 1) % NX, y, z, c)
    other = device(x, y, z, 1 - c)
    my_head = y * NZ + z

    kv = (kbuf, vbuf)

    def slab(xx, zz):
        return ((c * NX + xx) * NZ + zz) * NY

    barrier = pltpu.get_barrier_semaphore()

    def greet(to):
        pl.semaphore_signal(barrier, inc=1, device_id=to, device_id_type=MESH)

    for dy in range(NY):
        for dz in range(NZ):
            if dy or dz:
                greet(device(x, (y + dy) % NY, (z + dz) % NZ, c))
    greet(right)
    greet(left)
    greet(other)
    greet(device(x, y, z + 1 - 2 * z_lo, 1 - c))
    pl.semaphore_wait(barrier, NY * NZ - 1 + 4)

    def target(t, zz, yy):
        return qbuf.at[zz * NY + yy] if t == 2 else kv[t].at[slab(x, zz) + yy]

    def piece(t, zz, yy):
        rows = (k_hbm, v_hbm, q_hbm)[t]
        return rows.at[:, pl.ds(pl.multiple_of((yy * NZ + zz) * BLOCK, BLOCK), BLOCK)]

    def send_near(t):
        for dy in (1, 3, 2):
            yy = (y + dy) % NY
            sem = a_recv.at[t, 0] if t == 2 else near_recv.at[t, dy]
            remote(piece(t, z, yy), target(t, z, y), a_send.at[t], sem, device(x, yy, z, c))
        sem = a_recv.at[t, 0] if t == 2 else near_recv.at[t, 0]
        pltpu.make_async_copy(piece(t, z, y), target(t, z, y), sem).start()

    def send(t, g, ways):
        zz = (z + dz_of(g)) % NZ
        for dy in ways:
            yy = (y + dy) % NY
            remote(piece(t, zz, yy), target(t, z, y), a_send.at[t], a_recv.at[t, g], device(x, yy, zz, c))

    def send_all(t, first, ways):
        lax.fori_loop(first, NZ, lambda g, _: (send(t, g, ways), 0)[1], 0)

    def from_z(g):
        return (z + NZ - dz_of(g)) % NZ

    def to_both(src, dst, t, g):
        remote(src, dst, x_send.at[0], left_recv.at[t, g], right)
        remote(src, dst, x_send.at[1], right_recv.at[t, g], left)

    def gather_own_block(t):
        to_both(piece(t, z, y), kv[t].at[slab(x, z) + y], t, 0)

    def gather_near_block(t, dy):
        block = kv[t].at[slab(x, z) + (y + NY - dy) % NY]
        wait(block, near_recv.at[t, dy])
        to_both(block, block, t, 0)

    def swap_own_plane(t):
        wait(kv[t].at[slab(x, z) + y], near_recv.at[t, 0])
        own = kv[t].at[pl.ds(slab(x, z), NY)]
        remote(own, own, c_send, c_recv.at[t], other)

    def take_own(t, g):
        own = kv[t].at[pl.ds(slab(x, from_z(g)), NY)]
        wait(own, a_recv.at[t, g])
        to_both(own, own, t, g)
        remote(own, own, c_send, c_recv.at[t], other)

    def take_sides(t, g):
        base = slab((x + NX - 1) % NX, from_z(g))
        chunk = kv[t].at[pl.ds(base, NY)]
        half = kv[t].at[pl.ds(base, NY // 2)]
        wait(chunk, left_recv.at[t, g])
        remote(half, half, x_send.at[2], far_recv.at[t, g], right)
        remote(chunk, chunk, c_send, c_recv.at[t], other)
        base = slab((x + 1) % NX, from_z(g))
        chunk = kv[t].at[pl.ds(base, NY)]
        half = kv[t].at[pl.ds(base + NY // 2, NY // 2)]
        wait(chunk, right_recv.at[t, g])
        remote(half, half, x_send.at[2], far_recv.at[t, g], left)
        remote(chunk, chunk, c_send, c_recv.at[t], other)

    def take_far(t, g):
        chunk = kv[t].at[pl.ds(slab((x + 2) % NX, from_z(g)), NY)]
        wait(chunk, far_recv.at[t, g])
        remote(chunk, chunk, c_send, c_recv.at[t], other)

    def places_of(zz, yy):
        row = (yy * (NZ // 2) + zz // 2) * 2 + c
        return [slots[zz % 2, j, row] for j in range(LIVE)]

    def score(zz, yy):
        n = zz * NY + yy
        keys = jnp.concatenate([kbuf[p] for p in places_of(zz, yy)], axis=0)
        s = lax.dot_general(qbuf[n], keys, (((1,), (1,)), ((), ())), preferred_element_type=jnp.float32)
        m = jnp.max(s, axis=1, keepdims=True)
        p = jnp.exp2((s - m) * EXP_SCALE)
        weights[n] = p.astype(jnp.bfloat16)
        totals[n] = jnp.broadcast_to(jnp.sum(p, axis=1, keepdims=True), (BLOCK, BLOCK))

    def mix(zz, yy):
        n = zz * NY + yy
        values = jnp.concatenate([vbuf[p] for p in places_of(zz, yy)], axis=0)
        o = lax.dot_general(weights[n], values, (((1,), (0,)), ((), ())), preferred_element_type=jnp.float32)
        obuf[n] = (o / totals[n]).astype(jnp.bfloat16)
        return obuf.at[n]

    gather_own_block(0)
    send_near(0)
    gather_own_block(1)
    send_near(1)
    for g in range(1, 5):
        send(0, g, (0,))

    owner_z = z_hi * 2 + c
    remote(lists_hbm.at[0], lists_v.at[z_lo], l_send, l_recv, device(x, y, owner_z, 1 - c))

    @pl.when(z_lo == c)
    def _():
        pltpu.make_async_copy(lists_hbm.at[0], lists_v.at[z_lo], l_recv).start()

    @pl.when(z_lo != c)
    def _():
        remote(lists_hbm.at[0], lists_v.at[z_lo], l_send, l_recv, device(x, y, owner_z, c))

    gather_near_block(0, 1)
    gather_near_block(0, 3)
    send(0, 1, (1, 3, 2))
    send(0, 2, (1, 3, 2))
    gather_near_block(0, 2)
    swap_own_plane(0)
    gather_near_block(1, 1)
    gather_near_block(1, 3)
    send(0, 3, (1, 3, 2))
    send(0, 4, (1, 3, 2))
    gather_near_block(1, 2)
    swap_own_plane(1)
    send(0, 5, (0, 1, 3, 2))
    send(0, 6, (0, 1, 3, 2))
    take_own(0, 1)
    take_sides(0, 0)
    send(0, 7, (0, 1, 3, 2))
    send_all(1, 1, (0, 1, 3, 2))
    take_own(0, 2)
    take_sides(1, 0)
    send_near(2)
    send_all(2, 1, (0, 1, 3, 2))
    take_own(0, 3)
    take_sides(0, 1)
    take_far(0, 0)
    take_own(0, 4)
    take_sides(0, 2)
    take_far(1, 0)

    def keys(g, _):
        take_own(0, g + 4)
        take_sides(0, g + 2)
        take_far(0, g)
        return 0

    lax.fori_loop(1, 4, keys, 0)

    def both(g, _):
        take_own(1, g)
        take_sides(0, g + 5)
        take_far(0, g + 3)
        return 0

    lax.fori_loop(1, 3, both, 0)

    def values(g, _):
        take_own(1, g + 2)
        take_sides(1, g)
        take_far(0, g + 5)
        return 0

    lax.fori_loop(1, 3, values, 0)

    wait(lists_v, l_recv)
    i = lists_v[...]
    slots_v[...] = (((i & 1) * NX + ((i >> 5) & 3)) * NZ + ((i >> 1) & 3) * 2 + (i >> 7)) * NY + ((i >> 3) & 3)
    to_smem = pltpu.make_async_copy(slots_v, slots, s_sem)
    to_smem.start()
    to_smem.wait()

    wait(kbuf.at[pl.ds((1 - c) * HALF, HALF)], c_recv.at[0])

    def score_and_gather(g, _):
        @pl.when(g < 3)
        def _():
            take_own(1, g + 5)

        @pl.when(g < 5)
        def _():
            take_sides(1, g + 3)

        @pl.when(g < 7)
        def _():
            take_far(1, g + 1)

        zz = from_z(g)
        wait(qbuf.at[pl.ds(zz * NY, NY)], a_recv.at[2, g])
        for yy in range(NY):
            score(zz, yy)
        return 0

    lax.fori_loop(0, NZ, score_and_gather, 0)
    wait(vbuf.at[pl.ds((1 - c) * HALF, HALF)], c_recv.at[1])

    mine = out_hbm.at[:, pl.ds(pl.multiple_of(my_head * BLOCK, BLOCK), BLOCK)]

    def pair(p, _):
        near, r = p - 14, p - 2
        dz_a = jnp.where(p < 2, 4, jnp.where(p < 14, 3 - r // 4, 0))
        dz_b = (NZ - dz_a) % NZ
        dy_a = jnp.where(p < 2, 2 * p, jnp.where(p < 14, (r + NY) % NY, 1 + near))
        dy_b = jnp.where(p < 2, 2 * p + 1, jnp.where(p < 14, (r + NY) % NY, (3 - 3 * near + NY) % NY))
        yy_a, zz_a, yy_b, zz_b = (y + dy_a) % NY, (z + dz_a) % NZ, (y + dy_b) % NY, (z + dz_b) % NZ
        src_a = mix(zz_a, yy_a)
        src_b = mix(zz_b, yy_b)
        remote(src_a, mine, o_send, o_recv, device(x, yy_a, zz_a, c))

        @pl.when(p < 15)
        def _():
            remote(src_b, mine, o_send, o_recv, device(x, yy_b, zz_b, c))

        @pl.when(p == 15)
        def _():
            pltpu.make_async_copy(src_b, mine, o_recv).start()

        return 0

    lax.fori_loop(0, 16, pair, 0)

    for t in range(3):
        wait(kbuf.at[pl.ds(0, NY * NZ - 1)], a_send.at[t])
    for i in range(3):
        wait(kbuf.at[pl.ds(0, 2 * NZ * NY)], x_send.at[i])
    wait(kbuf, c_send)
    wait(lists_v.at[0], l_send)

    @pl.when(z_lo != c)
    def _():
        wait(lists_v.at[0], l_send)

    wait(obuf.at[pl.ds(0, NY * NZ - 1)], o_send)
    wait(out_hbm, o_recv)


def on_device(query_rows, key_rows, value_rows, block_lists):
    dma = pltpu.SemaphoreType.DMA
    return pl.pallas_call(
        kernel,
        out_shape=jax.ShapeDtypeStruct(query_rows.shape, jnp.bfloat16),
        in_specs=[pl.BlockSpec(memory_space=pl.ANY)] * 4,
        out_specs=pl.BlockSpec(memory_space=pl.ANY),
        scratch_shapes=[
            pltpu.VMEM((2 * HALF, BLOCK, BLOCK), jnp.bfloat16),
            pltpu.VMEM((2 * HALF, BLOCK, BLOCK), jnp.bfloat16),
            pltpu.VMEM((NY * NZ, BLOCK, BLOCK), jnp.bfloat16),
            pltpu.VMEM((NY * NZ, BLOCK, BLOCK), jnp.bfloat16),
            pltpu.VMEM((NY * NZ, BLOCK, LIVE * BLOCK), jnp.bfloat16),
            pltpu.VMEM((NY * NZ, BLOCK, BLOCK), jnp.float32),
            pltpu.VMEM((2, LIVE, 32), jnp.int32),
            pltpu.VMEM((2, LIVE, 32), jnp.int32),
            pltpu.SMEM((2, LIVE, 32), jnp.int32),
            dma((3,)), dma((2, NY)), dma((3, NZ)), dma((3,)), dma((2, NZ)), dma((2, NZ)), dma((2, NZ)), dma, dma((2,)),
            dma, dma, dma, dma, dma,
        ],
        compiler_params=pltpu.CompilerParams(collective_id=0, has_side_effects=True, vmem_limit_bytes=52 * 2**20),
        name="attention",
    )(query_rows, key_rows, value_rows, jnp.swapaxes(block_lists, 1, 2))


def solution(mesh):
    in_specs = (P(("blk", "head"), None), P(("blk", "head"), None), P(("blk", "head"), None), P("head", "blk", None))
    return jax.shard_map(
        on_device, mesh=mesh, in_specs=in_specs, out_specs=P(("blk", "head"), None), check_vma=False
    )
```

```python
import math

import jax
import jax.numpy as jnp
from jax import lax
from jax.experimental import pallas as pl
from jax.experimental.pallas import tpu as pltpu
from jax.sharding import PartitionSpec as P

MESH = pl.DeviceIdType.MESH
BLOCK = 128
LIVE = 16
NX, NY, NZ = 4, 4, 8
SLABS = NX * NY * NZ
HALF = BLOCK // 2
EXP_SCALE = (128**-0.5) * math.log2(math.e)


def device(x, y, z, c):
    return ((z % 2) * NX + x, (y * (NZ // 2) + z // 2) * 2 + c)


def dz_of(g):
    return jnp.where(g % 2 == 1, (g + 1) // 2, (NZ - g // 2) % NZ)


def far_first(i):
    return jnp.clip(jnp.where(i % 2 == 1, NZ - 2 - i, NZ - i), 0, NZ - 1)


def remote(src, dst, send_sem, recv_sem, to):
    copy = pltpu.make_async_remote_copy(
        src_ref=src, dst_ref=dst, send_sem=send_sem, recv_sem=recv_sem, device_id=to, device_id_type=MESH
    )
    copy.start()


def wait(ref, sem):
    pltpu.make_async_copy(ref, ref, sem).wait()


def kernel(
    q_hbm, k_hbm, v_hbm, lists_hbm, out_hbm,
    kbuf, lobuf, hibuf, qbuf, vraw, lo_out, hi_out, weights, totals, mixed, landed, obuf, lists_v, slots_v, slots,
    v_sem, a_send, near_recv, a_recv, x_send, left_recv, right_recv, far_recv, c_send, c_recv,
    l_send, l_recv, s_sem, o_send, o_recv, f_sem,
):
    blk, head = lax.axis_index("blk"), lax.axis_index("head")
    x, z_lo = blk % NX, blk // NX
    y, z_hi, c = head // NZ, (head // 2) % (NZ // 2), head % 2
    z = z_hi * 2 + z_lo
    right, left = device((x + 1) % NX, y, z, c), device((x + NX - 1) % NX, y, z, c)
    other = device(x, y, z, 1 - c)

    kv = (kbuf, lobuf, hibuf)
    low_lanes = lax.broadcasted_iota(jnp.int32, (HALF, BLOCK), 1) < HALF

    def slab(xx, zz):
        return ((c * NX + xx) * NZ + zz) * NY

    load_v = pltpu.make_async_copy(v_hbm, vraw, v_sem)
    load_v.start()

    barrier = pltpu.get_barrier_semaphore()

    def greet(to):
        pl.semaphore_signal(barrier, inc=1, device_id=to, device_id_type=MESH)

    for dy in range(NY):
        for dz in range(NZ):
            if dy or dz:
                greet(device(x, (y + dy) % NY, (z + dz) % NZ, c))
    greet(right)
    greet(left)
    greet(other)
    greet(device(x, y, z + 1 - 2 * z_lo, 1 - c))
    def pack(h, _):
        columns = pl.ds(pl.multiple_of(h * BLOCK, BLOCK), BLOCK)
        top = vraw[0:HALF, columns].astype(jnp.float32)
        bottom = vraw[HALF:BLOCK, columns].astype(jnp.float32)
        lo_out[h] = jnp.where(low_lanes, top, pltpu.roll(bottom, HALF, 1)).astype(jnp.bfloat16)
        hi_out[h] = jnp.where(low_lanes, pltpu.roll(top, HALF, 1), bottom).astype(jnp.bfloat16)
        return 0

    load_v.wait()
    lax.fori_loop(0, NY * NZ // 2, lambda i, _: pack(2 * i + 1, pack(2 * i, 0)), 0)
    pl.semaphore_wait(barrier, NY * NZ - 1 + 4)

    def target(t, zz, yy):
        return qbuf.at[zz * NY + yy] if t == 3 else kv[t].at[slab(x, zz) + yy]

    def piece(t, zz, yy):
        if t in (1, 2):
            return (lo_out, hi_out)[t - 1].at[yy * NZ + zz]
        rows = q_hbm if t == 3 else k_hbm
        return rows.at[:, pl.ds(pl.multiple_of((yy * NZ + zz) * BLOCK, BLOCK), BLOCK)]

    def send_near(t):
        for dy in (1, 3, 2):
            yy = (y + dy) % NY
            sem = a_recv.at[t, 0] if t else near_recv.at[dy]
            remote(piece(t, z, yy), target(t, z, y), a_send.at[t], sem, device(x, yy, z, c))
        sem = a_recv.at[t, 0] if t else near_recv.at[0]
        pltpu.make_async_copy(piece(t, z, y), target(t, z, y), sem).start()

    def send(t, g, ways):
        zz = (z + dz_of(g)) % NZ
        for dy in ways:
            yy = (y + dy) % NY
            remote(piece(t, zz, yy), target(t, z, y), a_send.at[t], a_recv.at[t, g], device(x, yy, zz, c))

    def send_all(t, first, ways):
        lax.fori_loop(first, NZ, lambda g, _: (send(t, g, ways), 0)[1], 0)

    def from_z(g):
        return (z + NZ - dz_of(g)) % NZ

    def to_both(src, dst, t, g):
        remote(src, dst, x_send.at[0], left_recv.at[t, g], right)
        remote(src, dst, x_send.at[1], right_recv.at[t, g], left)

    def gather_near_block(dy):
        block = kbuf.at[slab(x, z) + (y + NY - dy) % NY]
        wait(block, near_recv.at[dy])
        to_both(block, block, 0, 0)

    def swap_own_plane():
        wait(kbuf.at[slab(x, z) + y], near_recv.at[0])
        own = kbuf.at[pl.ds(slab(x, z), NY)]
        remote(own, own, c_send, c_recv.at[0], other)

    def take_own(t, g):
        own = kv[t].at[pl.ds(slab(x, from_z(g)), NY)]
        wait(own, a_recv.at[t, g])
        to_both(own, own, t, g)
        remote(own, own, c_send, c_recv.at[t], other)

    def take_sides(t, g):
        base = slab((x + NX - 1) % NX, from_z(g))
        chunk = kv[t].at[pl.ds(base, NY)]
        half = kv[t].at[pl.ds(base, NY // 2)]
        wait(chunk, left_recv.at[t, g])
        remote(half, half, x_send.at[2], far_recv.at[t, g], right)
        remote(chunk, chunk, c_send, c_recv.at[t], other)
        base = slab((x + 1) % NX, from_z(g))
        chunk = kv[t].at[pl.ds(base, NY)]
        half = kv[t].at[pl.ds(base + NY // 2, NY // 2)]
        wait(chunk, right_recv.at[t, g])
        remote(half, half, x_send.at[2], far_recv.at[t, g], left)
        remote(chunk, chunk, c_send, c_recv.at[t], other)

    def take_far(t, g):
        chunk = kv[t].at[pl.ds(slab((x + 2) % NX, from_z(g)), NY)]
        wait(chunk, far_recv.at[t, g])
        remote(chunk, chunk, c_send, c_recv.at[t], other)

    def from_other_core(t):
        wait(kv[t].at[pl.ds((1 - c) * SLABS, SLABS)], c_recv.at[t])

    def places_of(zz, yy):
        row = (yy * (NZ // 2) + zz // 2) * 2 + c
        return [slots[zz % 2, j, row] for j in range(LIVE)]

    def score(zz, yy):
        n = zz * NY + yy
        places = places_of(zz, yy)
        keys = [kbuf[p, 0:HALF] for p in places] + [kbuf[p, HALF:BLOCK] for p in places]
        s = lax.dot_general(
            qbuf[n], jnp.concatenate(keys, axis=0), (((1,), (1,)), ((), ())), preferred_element_type=jnp.float32
        )
        m = jnp.max(s, axis=1, keepdims=True)
        p = jnp.exp2((s - m) * EXP_SCALE)
        weights[n, 0:BLOCK] = p[:, : LIVE * HALF].astype(jnp.bfloat16)
        weights[n, BLOCK : 2 * BLOCK] = p[:, LIVE * HALF :].astype(jnp.bfloat16)
        total = jnp.broadcast_to(jnp.sum(p, axis=1, keepdims=True), (BLOCK, BLOCK))
        totals[n] = jnp.where(low_lanes, total[0:HALF], total[HALF:BLOCK])

    def mix(half, zz, yy):
        n = zz * NY + yy
        values = jnp.concatenate([kv[1 + half][p] for p in places_of(zz, yy)], axis=0)
        o = lax.dot_general(weights[n], values, (((1,), (0,)), ((), ())), preferred_element_type=jnp.float32)
        straight = jnp.where(low_lanes, o[0:HALF], o[3 * HALF : 4 * HALF])
        crossed = jnp.where(low_lanes, o[HALF : 2 * HALF], o[2 * HALF : 3 * HALF])
        mixed[half, n] = ((straight + pltpu.roll(crossed, HALF, 1)) / totals[n]).astype(jnp.bfloat16)
        return mixed.at[half, n]

    def mix_group(half, g):
        zz = from_z(g)
        ways = (1, 3, 2, 0)
        made = [mix(half, zz, (y + dy) % NY) for dy in ways]
        place = landed.at[half, z * NY + y]
        for dy, src in zip(ways, made):
            to = device(x, (y + dy) % NY, zz, c)
            if dy:
                remote(src, place, o_send.at[half], o_recv.at[half, g], to)
                continue

            @pl.when(g > 0)
            def _(src=src, to=to):
                remote(src, place, o_send.at[half], o_recv.at[half, g], to)

            @pl.when(g == 0)
            def _(src=src):
                pltpu.make_async_copy(src, place, o_recv.at[half, g]).start()

    to_both(piece(0, z, y), kbuf.at[slab(x, z) + y], 0, 0)
    for t in range(3):
        send_near(t)
    send_all(0, 1, (0,))

    owner_z = z_hi * 2 + c
    remote(lists_hbm.at[0], lists_v.at[z_lo], l_send, l_recv, device(x, y, owner_z, 1 - c))

    @pl.when(z_lo == c)
    def _():
        pltpu.make_async_copy(lists_hbm.at[0], lists_v.at[z_lo], l_recv).start()

    @pl.when(z_lo != c)
    def _():
        remote(lists_hbm.at[0], lists_v.at[z_lo], l_send, l_recv, device(x, y, owner_z, c))

    def step(count, *takes):
        def body(g, _):
            for take, t, ahead in takes:
                take(t, g + ahead)
            return 0

        lax.fori_loop(0, count, body, 0)

    gather_near_block(1)
    gather_near_block(3)
    send(0, 1, (1, 3, 2))
    send(0, 2, (1, 3, 2))
    gather_near_block(2)
    swap_own_plane()
    take_own(1, 0)
    send(0, 3, (1, 3, 2))
    send(0, 4, (1, 3, 2))
    take_own(2, 0)
    send(0, 5, (1, 3, 2))
    send(0, 6, (1, 3, 2))
    take_own(0, 1)
    take_sides(0, 0)
    send(0, 7, (1, 3, 2))
    send_all(1, 1, (0, 1, 3, 2))
    take_own(0, 2)
    take_sides(1, 0)
    send_near(3)
    lax.fori_loop(1, 5, lambda g, _: (send(3, g, (0, 1, 3, 2)), 0)[1], 0)
    take_own(0, 3)
    take_sides(2, 0)
    take_far(0, 0)
    send_all(2, 1, (0, 1, 3, 2))
    send_all(3, 5, (0, 1, 3, 2))
    take_own(0, 4)
    take_sides(0, 1)
    take_far(1, 0)
    take_sides(0, 2)
    take_far(2, 0)
    step(3, (take_own, 0, 5), (take_sides, 0, 3), (take_far, 0, 1))
    step(2, (take_own, 1, 1), (take_sides, 0, 6), (take_far, 0, 4))
    step(2, (take_own, 1, 3), (take_sides, 1, 1), (take_far, 0, 6))

    wait(lists_v, l_recv)
    i = lists_v[...]
    slots_v[...] = (((i & 1) * NX + ((i >> 5) & 3)) * NZ + ((i >> 1) & 3) * 2 + (i >> 7)) * NY + ((i >> 3) & 3)
    to_smem = pltpu.make_async_copy(slots_v, slots, s_sem)
    to_smem.start()
    to_smem.wait()
    from_other_core(0)

    def planned(i, plan):
        for number, takes in enumerate(plan):
            if takes:

                @pl.when(i == number)
                def _(takes=takes):
                    for take, t, *groups in takes:
                        for group in groups:
                            take(t, jnp.int32(group))

    def score_group(g):
        zz = from_z(g)
        wait(qbuf.at[pl.ds(zz * NY, NY)], a_recv.at[3, g])
        for yy in range(NY):
            score(zz, yy)

    def score_step(g, _):
        planned(
            g,
            (
                ((take_own, 1, 5), (take_sides, 1, 3), (take_far, 1, 1)),
                ((take_own, 1, 6), (take_sides, 1, 4), (take_far, 1, 2)),
                ((take_own, 1, 7), (take_sides, 1, 5), (take_far, 1, 3)),
                ((take_own, 2, 1), (take_sides, 1, 6), (take_far, 1, 4)),
                ((take_own, 2, 2), (take_sides, 1, 7), (take_far, 1, 5)),
            ),
        )
        score_group(g)
        return 0

    lax.fori_loop(0, 5, score_step, 0)
    take_own(2, 3)
    take_far(1, 6)
    take_own(2, 4)
    take_far(1, 7)
    from_other_core(1)

    def low_step(i, _):
        planned(
            i,
            (
                ((take_sides, 2, 1), (take_own, 2, 5)),
                ((take_sides, 2, 2), (take_own, 2, 6, 7)),
                ((take_sides, 2, 3),),
                ((take_sides, 2, 4), (take_far, 2, 1)),
                ((take_sides, 2, 5),),
                ((take_sides, 2, 6), (take_far, 2, 2)),
                ((take_sides, 2, 7), (take_far, 2, 3)),
                ((take_far, 2, 4),),
            ),
        )
        g = jnp.where(i < 4, i + 3, jnp.where(i == 4, 1, jnp.where(i == 5, 7, jnp.where(i == 6, 2, 0))))

        @pl.when((i == 2) | (i == 3) | (i == 5))
        def _():
            score_group(g)

        mix_group(0, g)
        return 0

    lax.fori_loop(0, NZ, low_step, 0)
    step(3, (take_far, 2, 5))
    from_other_core(2)

    lax.fori_loop(0, NZ, lambda i, _: (mix_group(1, far_first(i)), 0)[1], 0)

    def unpack(i, _):
        g = far_first(i)
        zz = (z + dz_of(g)) % NZ
        for half in range(2):
            wait(landed.at[half, pl.ds(zz * NY, NY)], o_recv.at[half, g])
        for yy in range(NY):
            n = zz * NY + yy
            lo, hi = landed[0, n].astype(jnp.float32), landed[1, n].astype(jnp.float32)
            obuf[n, 0:HALF] = jnp.where(low_lanes, lo, pltpu.roll(hi, HALF, 1)).astype(jnp.bfloat16)
            obuf[n, HALF:BLOCK] = jnp.where(low_lanes, pltpu.roll(lo, HALF, 1), hi).astype(jnp.bfloat16)
            columns = pl.ds(pl.multiple_of((yy * NZ + zz) * BLOCK, BLOCK), BLOCK)
            pltpu.make_async_copy(obuf.at[n], out_hbm.at[:, columns], f_sem).start()
        return 0

    lax.fori_loop(0, NZ, unpack, 0)

    for t in range(4):
        wait(kv[t % 3].at[pl.ds(0, NY * NZ - 1)], a_send.at[t])
    for i in range(3):
        wait(kbuf.at[pl.ds(0, 2 * NZ * NY)], x_send.at[i])
    wait(kbuf, c_send)
    wait(lists_v.at[0], l_send)

    @pl.when(z_lo != c)
    def _():
        wait(lists_v.at[0], l_send)

    for half in range(2):
        wait(mixed.at[half, pl.ds(0, NY * NZ - 1)], o_send.at[half])
    wait(out_hbm, f_sem)


def on_device(query_rows, key_rows, value_rows, block_lists):
    dma = pltpu.SemaphoreType.DMA
    return pl.pallas_call(
        kernel,
        out_shape=jax.ShapeDtypeStruct(query_rows.shape, jnp.bfloat16),
        in_specs=[pl.BlockSpec(memory_space=pl.ANY)] * 4,
        out_specs=pl.BlockSpec(memory_space=pl.ANY),
        scratch_shapes=[
            pltpu.VMEM((2 * SLABS, BLOCK, BLOCK), jnp.bfloat16),
            pltpu.VMEM((2 * SLABS, HALF, BLOCK), jnp.bfloat16),
            pltpu.VMEM((2 * SLABS, HALF, BLOCK), jnp.bfloat16),
            pltpu.VMEM((NY * NZ, BLOCK, BLOCK), jnp.bfloat16),
            pltpu.VMEM(value_rows.shape, jnp.bfloat16),
            pltpu.VMEM((NY * NZ, HALF, BLOCK), jnp.bfloat16),
            pltpu.VMEM((NY * NZ, HALF, BLOCK), jnp.bfloat16),
            pltpu.VMEM((NY * NZ, 2 * BLOCK, LIVE * HALF), jnp.bfloat16),
            pltpu.VMEM((NY * NZ, HALF, BLOCK), jnp.float32),
            pltpu.VMEM((2, NY * NZ, HALF, BLOCK), jnp.bfloat16),
            pltpu.VMEM((2, NY * NZ, HALF, BLOCK), jnp.bfloat16),
            pltpu.VMEM((NY * NZ, BLOCK, BLOCK), jnp.bfloat16),
            pltpu.VMEM((2, LIVE, 32), jnp.int32),
            pltpu.VMEM((2, LIVE, 32), jnp.int32),
            pltpu.SMEM((2, LIVE, 32), jnp.int32),
            dma, dma((4,)), dma((NY,)), dma((4, NZ)), dma((3,)), dma((3, NZ)), dma((3, NZ)), dma((3, NZ)), dma, dma((3,)),
            dma, dma, dma, dma((2,)), dma((2, NZ)), dma,
        ],
        compiler_params=pltpu.CompilerParams(collective_id=0, has_side_effects=True, vmem_limit_bytes=52 * 2**20),
        name="attention",
    )(query_rows, key_rows, value_rows, jnp.swapaxes(block_lists, 1, 2))


def solution(mesh):
    in_specs = (P(("blk", "head"), None), P(("blk", "head"), None), P(("blk", "head"), None), P("head", "blk", None))
    return jax.shard_map(
        on_device, mesh=mesh, in_specs=in_specs, out_specs=P(("blk", "head"), None), check_vma=False
    )
```

```python
import math

import jax
import jax.numpy as jnp
from jax import lax
from jax.experimental import pallas as pl
from jax.experimental.pallas import tpu as pltpu
from jax.sharding import PartitionSpec as P

MESH = pl.DeviceIdType.MESH
BLOCK = 128
LIVE = 16
NX, NY, NZ = 4, 4, 8
SLABS = NX * NY * NZ
HALF = BLOCK // 2
EXP_SCALE = (128**-0.5) * math.log2(math.e)


def device(x, y, z, c):
    return ((z % 2) * NX + x, (y * (NZ // 2) + z // 2) * 2 + c)


def dz_of(g):
    return jnp.where(g % 2 == 1, (g + 1) // 2, (NZ - g // 2) % NZ)


def far_first(i):
    return jnp.clip(jnp.where(i % 2 == 1, NZ - 2 - i, NZ - i), 0, NZ - 1)


def remote(src, dst, send_sem, recv_sem, to):
    copy = pltpu.make_async_remote_copy(
        src_ref=src, dst_ref=dst, send_sem=send_sem, recv_sem=recv_sem, device_id=to, device_id_type=MESH
    )
    copy.start()


def wait(ref, sem):
    pltpu.make_async_copy(ref, ref, sem).wait()


def kernel(
    q_hbm, k_hbm, v_hbm, lists_hbm, out_ref,
    kbuf, lobuf, hibuf, qbuf, vraw, lo_out, hi_out, weights, totals, mixed, landed, lists_v, slots_v, slots,
    v_sem, a_send, near_recv, a_recv, x_send, left_recv, right_recv, far_recv, c_send, c_recv,
    l_send, l_recv, s_sem, o_send, o_recv,
):
    blk, head = lax.axis_index("blk"), lax.axis_index("head")
    x, z_lo = blk % NX, blk // NX
    y, z_hi, c = head // NZ, (head // 2) % (NZ // 2), head % 2
    z = z_hi * 2 + z_lo
    right, left = device((x + 1) % NX, y, z, c), device((x + NX - 1) % NX, y, z, c)
    other = device(x, y, z, 1 - c)

    kv = (kbuf, lobuf, hibuf)
    low_lanes = lax.broadcasted_iota(jnp.int32, (HALF, BLOCK), 1) < HALF

    def slab(xx, zz):
        return ((c * NX + xx) * NZ + zz) * NY

    load_v = pltpu.make_async_copy(v_hbm, vraw, v_sem)
    load_v.start()

    barrier = pltpu.get_barrier_semaphore()

    def greet(to):
        pl.semaphore_signal(barrier, inc=1, device_id=to, device_id_type=MESH)

    for dy in range(NY):
        for dz in range(NZ):
            if dy or dz:
                greet(device(x, (y + dy) % NY, (z + dz) % NZ, c))
    greet(right)
    greet(left)
    greet(other)
    greet(device(x, y, z + 1 - 2 * z_lo, 1 - c))
    def pack(h, _):
        columns = pl.ds(pl.multiple_of(h * BLOCK, BLOCK), BLOCK)
        top = vraw[0:HALF, columns].astype(jnp.float32)
        bottom = vraw[HALF:BLOCK, columns].astype(jnp.float32)
        lo_out[h] = jnp.where(low_lanes, top, pltpu.roll(bottom, HALF, 1)).astype(jnp.bfloat16)
        hi_out[h] = jnp.where(low_lanes, pltpu.roll(top, HALF, 1), bottom).astype(jnp.bfloat16)
        return 0

    pl.semaphore_wait(barrier, NY * NZ - 1 + 4)

    def target(t, zz, yy):
        return qbuf.at[zz * NY + yy] if t == 3 else kv[t].at[slab(x, zz) + yy]

    def piece(t, zz, yy):
        if t in (1, 2):
            return (lo_out, hi_out)[t - 1].at[yy * NZ + zz]
        rows = q_hbm if t == 3 else k_hbm
        return rows.at[:, pl.ds(pl.multiple_of((yy * NZ + zz) * BLOCK, BLOCK), BLOCK)]

    def send_near(t):
        for dy in (1, 3, 2):
            yy = (y + dy) % NY
            sem = a_recv.at[t, 0] if t else near_recv.at[dy]
            remote(piece(t, z, yy), target(t, z, y), a_send.at[t], sem, device(x, yy, z, c))
        sem = a_recv.at[t, 0] if t else near_recv.at[0]
        pltpu.make_async_copy(piece(t, z, y), target(t, z, y), sem).start()

    def send(t, g, ways):
        zz = (z + dz_of(g)) % NZ
        for dy in ways:
            yy = (y + dy) % NY
            remote(piece(t, zz, yy), target(t, z, y), a_send.at[t], a_recv.at[t, g], device(x, yy, zz, c))

    def send_all(t, first, ways):
        lax.fori_loop(first, NZ, lambda g, _: (send(t, g, ways), 0)[1], 0)

    def from_z(g):
        return (z + NZ - dz_of(g)) % NZ

    def to_both(src, dst, t, g):
        remote(src, dst, x_send.at[0], left_recv.at[t, g], right)
        remote(src, dst, x_send.at[1], right_recv.at[t, g], left)

    def gather_near_block(dy):
        block = kbuf.at[slab(x, z) + (y + NY - dy) % NY]
        wait(block, near_recv.at[dy])
        to_both(block, block, 0, 0)

    def swap_own_plane():
        wait(kbuf.at[slab(x, z) + y], near_recv.at[0])
        own = kbuf.at[pl.ds(slab(x, z), NY)]
        remote(own, own, c_send, c_recv.at[0], other)

    def take_own(t, g):
        own = kv[t].at[pl.ds(slab(x, from_z(g)), NY)]
        wait(own, a_recv.at[t, g])
        to_both(own, own, t, g)
        remote(own, own, c_send, c_recv.at[t], other)

    def take_sides(t, g):
        base = slab((x + NX - 1) % NX, from_z(g))
        chunk = kv[t].at[pl.ds(base, NY)]
        half = kv[t].at[pl.ds(base, NY // 2)]
        wait(chunk, left_recv.at[t, g])
        remote(half, half, x_send.at[2], far_recv.at[t, g], right)
        remote(chunk, chunk, c_send, c_recv.at[t], other)
        base = slab((x + 1) % NX, from_z(g))
        chunk = kv[t].at[pl.ds(base, NY)]
        half = kv[t].at[pl.ds(base + NY // 2, NY // 2)]
        wait(chunk, right_recv.at[t, g])
        remote(half, half, x_send.at[2], far_recv.at[t, g], left)
        remote(chunk, chunk, c_send, c_recv.at[t], other)

    def take_far(t, g):
        chunk = kv[t].at[pl.ds(slab((x + 2) % NX, from_z(g)), NY)]
        wait(chunk, far_recv.at[t, g])
        remote(chunk, chunk, c_send, c_recv.at[t], other)

    def from_other_core(t):
        wait(kv[t].at[pl.ds((1 - c) * SLABS, SLABS)], c_recv.at[t])

    def places_of(zz, yy):
        row = (yy * (NZ // 2) + zz // 2) * 2 + c
        return [slots[zz % 2, j, row] for j in range(LIVE)]

    def score(zz, yy):
        n = zz * NY + yy
        places = places_of(zz, yy)
        keys = [kbuf[p, 0:HALF] for p in places] + [kbuf[p, HALF:BLOCK] for p in places]
        s = lax.dot_general(
            qbuf[n], jnp.concatenate(keys, axis=0), (((1,), (1,)), ((), ())), preferred_element_type=jnp.float32
        )
        m = jnp.max(s, axis=1, keepdims=True)
        p = jnp.exp2((s - m) * EXP_SCALE)
        weights[n, 0:BLOCK] = p[:, : LIVE * HALF].astype(jnp.bfloat16)
        weights[n, BLOCK : 2 * BLOCK] = p[:, LIVE * HALF :].astype(jnp.bfloat16)
        total = jnp.broadcast_to(jnp.sum(p, axis=1, keepdims=True), (BLOCK, BLOCK))
        totals[n] = jnp.where(low_lanes, total[0:HALF], total[HALF:BLOCK])

    def mix(half, zz, yy):
        n = zz * NY + yy
        values = jnp.concatenate([kv[1 + half][p] for p in places_of(zz, yy)], axis=0)
        o = lax.dot_general(weights[n], values, (((1,), (0,)), ((), ())), preferred_element_type=jnp.float32)
        straight = jnp.where(low_lanes, o[0:HALF], o[3 * HALF : 4 * HALF])
        crossed = jnp.where(low_lanes, o[HALF : 2 * HALF], o[2 * HALF : 3 * HALF])
        mixed[half, n] = ((straight + pltpu.roll(crossed, HALF, 1)) / totals[n]).astype(jnp.bfloat16)
        return mixed.at[half, n]

    def mix_group(half, g):
        zz = from_z(g)
        ways = (1, 3, 2, 0)
        made = [mix(half, zz, (y + dy) % NY) for dy in ways]
        place = landed.at[half, z * NY + y]
        for dy, src in zip(ways, made):
            to = device(x, (y + dy) % NY, zz, c)
            if dy:
                remote(src, place, o_send.at[half], o_recv.at[half, g], to)
                continue

            @pl.when(g > 0)
            def _(src=src, to=to):
                remote(src, place, o_send.at[half], o_recv.at[half, g], to)

            @pl.when(g == 0)
            def _(src=src):
                pltpu.make_async_copy(src, place, o_recv.at[half, g]).start()

    to_both(piece(0, z, y), kbuf.at[slab(x, z) + y], 0, 0)
    send_near(0)
    send_all(0, 1, (0, 1, 3, 2))
    load_v.wait()
    lax.fori_loop(0, NY * NZ // 2, lambda i, _: pack(2 * i + 1, pack(2 * i, 0)), 0)
    send_near(1)
    send_near(2)

    owner_z = z_hi * 2 + c
    remote(lists_hbm.at[0], lists_v.at[z_lo], l_send, l_recv, device(x, y, owner_z, 1 - c))

    @pl.when(z_lo == c)
    def _():
        pltpu.make_async_copy(lists_hbm.at[0], lists_v.at[z_lo], l_recv).start()

    @pl.when(z_lo != c)
    def _():
        remote(lists_hbm.at[0], lists_v.at[z_lo], l_send, l_recv, device(x, y, owner_z, c))

    def step(count, *takes):
        def body(g, _):
            for take, t, ahead in takes:
                take(t, g + ahead)
            return 0

        lax.fori_loop(0, count, body, 0)

    gather_near_block(1)
    gather_near_block(3)
    gather_near_block(2)
    swap_own_plane()
    take_own(1, 0)
    take_own(0, 1)
    take_sides(0, 0)
    send_all(1, 1, (0, 1, 3, 2))
    take_own(0, 2)
    take_sides(1, 0)
    send_near(3)
    lax.fori_loop(1, 5, lambda g, _: (send(3, g, (0, 1, 3, 2)), 0)[1], 0)
    take_own(0, 3)
    take_far(0, 0)
    send_all(2, 1, (0, 1, 3, 2))
    send_all(3, 5, (0, 1, 3, 2))
    take_own(0, 4)
    take_sides(0, 1)
    take_far(1, 0)
    take_sides(0, 2)
    step(3, (take_own, 0, 5), (take_sides, 0, 3), (take_far, 0, 1))
    step(2, (take_own, 1, 1), (take_sides, 0, 6), (take_far, 0, 4))
    step(2, (take_own, 1, 3), (take_sides, 1, 1), (take_far, 0, 6))

    wait(lists_v, l_recv)
    i = lists_v[...]
    slots_v[...] = (((i & 1) * NX + ((i >> 5) & 3)) * NZ + ((i >> 1) & 3) * 2 + (i >> 7)) * NY + ((i >> 3) & 3)
    to_smem = pltpu.make_async_copy(slots_v, slots, s_sem)
    to_smem.start()
    to_smem.wait()
    from_other_core(0)

    def planned(i, plan):
        for number, takes in enumerate(plan):
            if takes:

                @pl.when(i == number)
                def _(takes=takes):
                    for take, t, *groups in takes:
                        for group in groups:
                            take(t, jnp.int32(group))

    def score_group(g):
        zz = from_z(g)
        wait(qbuf.at[pl.ds(zz * NY, NY)], a_recv.at[3, g])
        for yy in range(NY):
            score(zz, yy)

    def score_step(g, _):
        planned(
            g,
            (
                ((take_own, 1, 5), (take_sides, 1, 3), (take_far, 1, 1)),
                ((take_own, 1, 6), (take_sides, 1, 4), (take_far, 1, 2)),
                ((take_own, 1, 7), (take_sides, 1, 5), (take_own, 2, 0), (take_far, 1, 3)),
                ((take_own, 2, 1), (take_sides, 1, 6), (take_far, 1, 4)),
                ((take_own, 2, 2), (take_sides, 1, 7), (take_far, 1, 5)),
            ),
        )
        score_group(g)
        return 0

    lax.fori_loop(0, 5, score_step, 0)
    take_own(2, 3)
    take_far(1, 6)
    take_sides(2, 0)
    take_own(2, 4)
    take_far(1, 7)
    from_other_core(1)

    def low_step(i, _):
        planned(
            i,
            (
                ((take_sides, 2, 1), (take_own, 2, 5)),
                ((take_sides, 2, 2), (take_own, 2, 6, 7)),
                ((take_sides, 2, 3),),
                ((take_sides, 2, 4), (take_far, 2, 0, 1)),
                ((take_sides, 2, 5),),
                ((take_sides, 2, 6), (take_far, 2, 2)),
                ((take_sides, 2, 7), (take_far, 2, 3)),
                ((take_far, 2, 4),),
            ),
        )
        g = jnp.where(i < 4, i + 3, jnp.where(i == 4, 1, jnp.where(i == 5, 7, jnp.where(i == 6, 2, 0))))

        @pl.when((i == 2) | (i == 3) | (i == 5))
        def _():
            score_group(g)

        mix_group(0, g)
        return 0

    lax.fori_loop(0, NZ, low_step, 0)
    step(3, (take_far, 2, 5))
    from_other_core(2)

    lax.fori_loop(0, NZ, lambda i, _: (mix_group(1, far_first(i)), 0)[1], 0)

    def unpack(i, _):
        g = far_first(i)
        zz = (z + dz_of(g)) % NZ
        for half in range(2):
            wait(landed.at[half, pl.ds(zz * NY, NY)], o_recv.at[half, g])
        for yy in range(NY):
            n = zz * NY + yy
            lo, hi = landed[0, n].astype(jnp.float32), landed[1, n].astype(jnp.float32)
            columns = pl.ds(pl.multiple_of((yy * NZ + zz) * BLOCK, BLOCK), BLOCK)
            out_ref[0:HALF, columns] = jnp.where(low_lanes, lo, pltpu.roll(hi, HALF, 1)).astype(jnp.bfloat16)
            out_ref[HALF:BLOCK, columns] = jnp.where(low_lanes, pltpu.roll(lo, HALF, 1), hi).astype(jnp.bfloat16)
        return 0

    lax.fori_loop(0, NZ, unpack, 0)

    for t in range(4):
        wait(kv[t % 3].at[pl.ds(0, NY * NZ - 1)], a_send.at[t])
    for i in range(3):
        wait(kbuf.at[pl.ds(0, 2 * NZ * NY)], x_send.at[i])
    wait(kbuf, c_send)
    wait(lists_v.at[0], l_send)

    @pl.when(z_lo != c)
    def _():
        wait(lists_v.at[0], l_send)

    for half in range(2):
        wait(mixed.at[half, pl.ds(0, NY * NZ - 1)], o_send.at[half])


def on_device(query_rows, key_rows, value_rows, block_lists):
    dma = pltpu.SemaphoreType.DMA
    return pl.pallas_call(
        kernel,
        out_shape=jax.ShapeDtypeStruct(query_rows.shape, jnp.bfloat16),
        in_specs=[pl.BlockSpec(memory_space=pl.ANY)] * 4,
        out_specs=pl.BlockSpec(memory_space=pltpu.VMEM),
        scratch_shapes=[
            pltpu.VMEM((2 * SLABS, BLOCK, BLOCK), jnp.bfloat16),
            pltpu.VMEM((2 * SLABS, HALF, BLOCK), jnp.bfloat16),
            pltpu.VMEM((2 * SLABS, HALF, BLOCK), jnp.bfloat16),
            pltpu.VMEM((NY * NZ, BLOCK, BLOCK), jnp.bfloat16),
            pltpu.VMEM(value_rows.shape, jnp.bfloat16),
            pltpu.VMEM((NY * NZ, HALF, BLOCK), jnp.bfloat16),
            pltpu.VMEM((NY * NZ, HALF, BLOCK), jnp.bfloat16),
            pltpu.VMEM((NY * NZ, 2 * BLOCK, LIVE * HALF), jnp.bfloat16),
            pltpu.VMEM((NY * NZ, HALF, BLOCK), jnp.float32),
            pltpu.VMEM((2, NY * NZ, HALF, BLOCK), jnp.bfloat16),
            pltpu.VMEM((2, NY * NZ, HALF, BLOCK), jnp.bfloat16),
            pltpu.VMEM((2, LIVE, 32), jnp.int32),
            pltpu.VMEM((2, LIVE, 32), jnp.int32),
            pltpu.SMEM((2, LIVE, 32), jnp.int32),
            dma, dma((4,)), dma((NY,)), dma((4, NZ)), dma((3,)), dma((3, NZ)), dma((3, NZ)), dma((3, NZ)), dma, dma((3,)),
            dma, dma, dma, dma((2,)), dma((2, NZ)),
        ],
        compiler_params=pltpu.CompilerParams(collective_id=0, has_side_effects=True, vmem_limit_bytes=52 * 2**20),
        name="attention",
    )(query_rows, key_rows, value_rows, jnp.swapaxes(block_lists, 1, 2))


def solution(mesh):
    in_specs = (P(("blk", "head"), None), P(("blk", "head"), None), P(("blk", "head"), None), P("head", "blk", None))
    return jax.shard_map(
        on_device, mesh=mesh, in_specs=in_specs, out_specs=P(("blk", "head"), None), check_vma=False
    )
```

```python
import math

import jax
import jax.numpy as jnp
from jax import lax
from jax.experimental import pallas as pl
from jax.experimental.pallas import tpu as pltpu
from jax.sharding import PartitionSpec as P

MESH = pl.DeviceIdType.MESH
BLOCK = 128
LIVE = 16
NX, NY, NZ = 4, 4, 8
SLABS = NX * NY * NZ
HALF = BLOCK // 2
EXP_SCALE = (128**-0.5) * math.log2(math.e)


def device(x, y, z, c):
    return ((z % 2) * NX + x, (y * (NZ // 2) + z // 2) * 2 + c)


def dz_of(g):
    return jnp.where(g % 2 == 1, (g + 1) // 2, (NZ - g // 2) % NZ)


def far_first(i):
    return jnp.clip(jnp.where(i % 2 == 1, NZ - 2 - i, NZ - i), 0, NZ - 1)


def remote(src, dst, send_sem, recv_sem, to):
    copy = pltpu.make_async_remote_copy(
        src_ref=src, dst_ref=dst, send_sem=send_sem, recv_sem=recv_sem, device_id=to, device_id_type=MESH
    )
    copy.start()


def wait(ref, sem):
    pltpu.make_async_copy(ref, ref, sem).wait()


def kernel(
    q_hbm, k_hbm, v_hbm, lists_hbm, out_ref,
    kbuf, lobuf, hibuf, qbuf, vraw, lo_out, hi_out, weights, totals, mixed, landed, lists_v, slots_v, slots,
    v_sem, a_send, near_recv, a_recv, x_send, left_recv, right_recv, far_recv, c_send, c_recv,
    l_send, l_recv, s_sem, o_send, o_recv,
):
    blk, head = lax.axis_index("blk"), lax.axis_index("head")
    x, z_lo = blk % NX, blk // NX
    y, z_hi, c = head // NZ, (head // 2) % (NZ // 2), head % 2
    z = z_hi * 2 + z_lo
    right, left = device((x + 1) % NX, y, z, c), device((x + NX - 1) % NX, y, z, c)
    other = device(x, y, z, 1 - c)

    kv = (kbuf, lobuf, hibuf)
    low_lanes = lax.broadcasted_iota(jnp.int32, (HALF, BLOCK), 1) < HALF

    def slab(xx, zz):
        return ((c * NX + xx) * NZ + zz) * NY

    load_v = pltpu.make_async_copy(v_hbm, vraw, v_sem)
    load_v.start()

    barrier = pltpu.get_barrier_semaphore()

    def greet(to):
        pl.semaphore_signal(barrier, inc=1, device_id=to, device_id_type=MESH)

    for dz in (4, 3, 5, 2, 6, 1, 7, 0):
        for dy in (2, 1, 3, 0):
            if dy or dz:
                greet(device(x, (y + dy) % NY, (z + dz) % NZ, c))
    greet(right)
    greet(left)
    greet(other)
    greet(device(x, y, z + 1 - 2 * z_lo, 1 - c))
    def pack(h, _):
        columns = pl.ds(pl.multiple_of(h * BLOCK, BLOCK), BLOCK)
        top = vraw[0:HALF, columns].astype(jnp.float32)
        bottom = vraw[HALF:BLOCK, columns].astype(jnp.float32)
        lo_out[h] = jnp.where(low_lanes, top, pltpu.roll(bottom, HALF, 1)).astype(jnp.bfloat16)
        hi_out[h] = jnp.where(low_lanes, pltpu.roll(top, HALF, 1), bottom).astype(jnp.bfloat16)
        return 0

    pl.semaphore_wait(barrier, NY * NZ - 1 + 4)

    def target(t, zz, yy):
        return qbuf.at[zz * NY + yy] if t == 3 else kv[t].at[slab(x, zz) + yy]

    def piece(t, zz, yy):
        if t in (1, 2):
            return (lo_out, hi_out)[t - 1].at[yy * NZ + zz]
        rows = q_hbm if t == 3 else k_hbm
        return rows.at[:, pl.ds(pl.multiple_of((yy * NZ + zz) * BLOCK, BLOCK), BLOCK)]

    def send_near(t):
        for dy in (1, 3, 2):
            yy = (y + dy) % NY
            sem = a_recv.at[t, 0] if t else near_recv.at[dy]
            remote(piece(t, z, yy), target(t, z, y), a_send.at[t], sem, device(x, yy, z, c))
        sem = a_recv.at[t, 0] if t else near_recv.at[0]
        pltpu.make_async_copy(piece(t, z, y), target(t, z, y), sem).start()

    def send(t, g, ways):
        zz = (z + dz_of(g)) % NZ
        for dy in ways:
            yy = (y + dy) % NY
            remote(piece(t, zz, yy), target(t, z, y), a_send.at[t], a_recv.at[t, g], device(x, yy, zz, c))

    def send_all(t, first, ways):
        lax.fori_loop(first, NZ, lambda g, _: (send(t, g, ways), 0)[1], 0)

    def from_z(g):
        return (z + NZ - dz_of(g)) % NZ

    def to_both(src, dst, t, g):
        remote(src, dst, x_send.at[0], left_recv.at[t, g], right)
        remote(src, dst, x_send.at[1], right_recv.at[t, g], left)

    def gather_near_block(dy):
        block = kbuf.at[slab(x, z) + (y + NY - dy) % NY]
        wait(block, near_recv.at[dy])
        to_both(block, block, 0, 0)

    def swap_own_plane():
        wait(kbuf.at[slab(x, z) + y], near_recv.at[0])
        own = kbuf.at[pl.ds(slab(x, z), NY)]
        remote(own, own, c_send, c_recv.at[0], other)

    def take_own(t, g):
        own = kv[t].at[pl.ds(slab(x, from_z(g)), NY)]
        wait(own, a_recv.at[t, g])
        to_both(own, own, t, g)
        remote(own, own, c_send, c_recv.at[t], other)

    def take_sides(t, g):
        base = slab((x + NX - 1) % NX, from_z(g))
        chunk = kv[t].at[pl.ds(base, NY)]
        half = kv[t].at[pl.ds(base, NY // 2)]
        wait(chunk, left_recv.at[t, g])
        remote(half, half, x_send.at[2], far_recv.at[t, g], right)
        remote(chunk, chunk, c_send, c_recv.at[t], other)
        base = slab((x + 1) % NX, from_z(g))
        chunk = kv[t].at[pl.ds(base, NY)]
        half = kv[t].at[pl.ds(base + NY // 2, NY // 2)]
        wait(chunk, right_recv.at[t, g])
        remote(half, half, x_send.at[2], far_recv.at[t, g], left)
        remote(chunk, chunk, c_send, c_recv.at[t], other)

    def take_far(t, g):
        chunk = kv[t].at[pl.ds(slab((x + 2) % NX, from_z(g)), NY)]
        wait(chunk, far_recv.at[t, g])
        remote(chunk, chunk, c_send, c_recv.at[t], other)

    def from_other_core(t):
        wait(kv[t].at[pl.ds((1 - c) * SLABS, SLABS)], c_recv.at[t])

    def places_of(zz, yy):
        row = (yy * (NZ // 2) + zz // 2) * 2 + c
        return [slots[zz % 2, j, row] for j in range(LIVE)]

    def score(zz, yy):
        n = zz * NY + yy
        places = places_of(zz, yy)
        keys = [kbuf[p, 0:HALF] for p in places] + [kbuf[p, HALF:BLOCK] for p in places]
        s = lax.dot_general(
            qbuf[n], jnp.concatenate(keys, axis=0), (((1,), (1,)), ((), ())), preferred_element_type=jnp.float32
        )
        m = jnp.max(s, axis=1, keepdims=True)
        p = jnp.exp2((s - m) * EXP_SCALE)
        weights[n, 0:BLOCK] = p[:, : LIVE * HALF].astype(jnp.bfloat16)
        weights[n, BLOCK : 2 * BLOCK] = p[:, LIVE * HALF :].astype(jnp.bfloat16)
        total = jnp.broadcast_to(jnp.sum(p, axis=1, keepdims=True), (BLOCK, BLOCK))
        totals[n] = jnp.where(low_lanes, total[0:HALF], total[HALF:BLOCK])

    def mix(half, zz, yy):
        n = zz * NY + yy
        values = jnp.concatenate([kv[1 + half][p] for p in places_of(zz, yy)], axis=0)
        o = lax.dot_general(weights[n], values, (((1,), (0,)), ((), ())), preferred_element_type=jnp.float32)
        straight = jnp.where(low_lanes, o[0:HALF], o[3 * HALF : 4 * HALF])
        crossed = jnp.where(low_lanes, o[HALF : 2 * HALF], o[2 * HALF : 3 * HALF])
        mixed[half, n] = ((straight + pltpu.roll(crossed, HALF, 1)) / totals[n]).astype(jnp.bfloat16)
        return mixed.at[half, n]

    def mix_group(half, g):
        zz = from_z(g)
        ways = (1, 3, 2, 0)
        made = [mix(half, zz, (y + dy) % NY) for dy in ways]
        place = landed.at[half, z * NY + y]
        for dy, src in zip(ways, made):
            to = device(x, (y + dy) % NY, zz, c)
            if dy:
                remote(src, place, o_send.at[half], o_recv.at[half, g], to)
                continue

            @pl.when(g > 0)
            def _(src=src, to=to):
                remote(src, place, o_send.at[half], o_recv.at[half, g], to)

            @pl.when(g == 0)
            def _(src=src):
                pltpu.make_async_copy(src, place, o_recv.at[half, g]).start()

    to_both(piece(0, z, y), kbuf.at[slab(x, z) + y], 0, 0)
    send_near(0)
    send_all(0, 1, (0, 1, 3, 2))
    load_v.wait()
    lax.fori_loop(0, NY * NZ // 2, lambda i, _: pack(2 * i + 1, pack(2 * i, 0)), 0)
    send_near(1)
    send_near(2)

    owner_z = z_hi * 2 + c
    remote(lists_hbm.at[0], lists_v.at[z_lo], l_send, l_recv, device(x, y, owner_z, 1 - c))

    @pl.when(z_lo == c)
    def _():
        pltpu.make_async_copy(lists_hbm.at[0], lists_v.at[z_lo], l_recv).start()

    @pl.when(z_lo != c)
    def _():
        remote(lists_hbm.at[0], lists_v.at[z_lo], l_send, l_recv, device(x, y, owner_z, c))

    def step(count, *takes):
        def body(g, _):
            for take, t, ahead in takes:
                take(t, g + ahead)
            return 0

        lax.fori_loop(0, count, body, 0)

    gather_near_block(1)
    gather_near_block(3)
    gather_near_block(2)
    swap_own_plane()
    take_own(1, 0)
    take_own(0, 1)
    take_sides(0, 0)
    send_all(1, 1, (0, 1, 3, 2))
    take_own(0, 2)
    take_sides(1, 0)
    send_near(3)
    lax.fori_loop(1, 5, lambda g, _: (send(3, g, (0, 1, 3, 2)), 0)[1], 0)
    take_own(0, 3)
    take_far(0, 0)
    send_all(2, 1, (0, 1, 3, 2))
    send_all(3, 5, (0, 1, 3, 2))
    take_own(0, 4)
    take_sides(0, 1)
    take_far(1, 0)
    take_sides(0, 2)
    step(3, (take_own, 0, 5), (take_sides, 0, 3), (take_far, 0, 1))
    step(2, (take_own, 1, 1), (take_sides, 0, 6), (take_far, 0, 4))
    step(2, (take_own, 1, 3), (take_sides, 1, 1), (take_far, 0, 6))

    wait(lists_v, l_recv)
    i = lists_v[...]
    slots_v[...] = (((i & 1) * NX + ((i >> 5) & 3)) * NZ + ((i >> 1) & 3) * 2 + (i >> 7)) * NY + ((i >> 3) & 3)
    to_smem = pltpu.make_async_copy(slots_v, slots, s_sem)
    to_smem.start()
    to_smem.wait()
    from_other_core(0)

    def planned(i, plan):
        for number, takes in enumerate(plan):
            if takes:

                @pl.when(i == number)
                def _(takes=takes):
                    for take, t, *groups in takes:
                        for group in groups:
                            take(t, jnp.int32(group))

    def score_group(g):
        zz = from_z(g)
        wait(qbuf.at[pl.ds(zz * NY, NY)], a_recv.at[3, g])
        for yy in range(NY):
            score(zz, yy)

    def score_step(g, _):
        planned(
            g,
            (
                ((take_own, 1, 5), (take_sides, 1, 3), (take_far, 1, 1)),
                ((take_own, 1, 6), (take_sides, 1, 4), (take_far, 1, 2)),
                ((take_own, 1, 7), (take_sides, 1, 5), (take_own, 2, 0), (take_far, 1, 3)),
                ((take_own, 2, 1), (take_sides, 1, 6), (take_far, 1, 4)),
                ((take_own, 2, 2), (take_sides, 1, 7), (take_far, 1, 5)),
            ),
        )
        score_group(g)
        return 0

    lax.fori_loop(0, 5, score_step, 0)
    take_own(2, 3)
    take_far(1, 6)
    take_sides(2, 0)
    take_own(2, 4)
    take_far(1, 7)
    from_other_core(1)

    def low_step(i, _):
        planned(
            i,
            (
                ((take_sides, 2, 1), (take_own, 2, 5)),
                ((take_sides, 2, 2), (take_own, 2, 6, 7)),
                ((take_sides, 2, 3),),
                ((take_sides, 2, 4), (take_far, 2, 0, 1)),
                ((take_sides, 2, 5),),
                ((take_sides, 2, 6), (take_far, 2, 2)),
                ((take_sides, 2, 7), (take_far, 2, 3)),
                ((take_far, 2, 4),),
            ),
        )
        g = jnp.where(i < 4, i + 3, jnp.where(i == 4, 1, jnp.where(i == 5, 7, jnp.where(i == 6, 2, 0))))

        @pl.when((i == 2) | (i == 3) | (i == 5))
        def _():
            score_group(g)

        mix_group(0, g)
        return 0

    lax.fori_loop(0, NZ, low_step, 0)
    step(3, (take_far, 2, 5))
    from_other_core(2)

    lax.fori_loop(0, NZ, lambda i, _: (mix_group(1, far_first(i)), 0)[1], 0)

    def unpack(i, _):
        g = far_first(i)
        zz = (z + dz_of(g)) % NZ
        for half in range(2):
            wait(landed.at[half, pl.ds(zz * NY, NY)], o_recv.at[half, g])
        for yy in range(NY):
            n = zz * NY + yy
            lo, hi = landed[0, n].astype(jnp.float32), landed[1, n].astype(jnp.float32)
            columns = pl.ds(pl.multiple_of((yy * NZ + zz) * BLOCK, BLOCK), BLOCK)
            out_ref[0:HALF, columns] = jnp.where(low_lanes, lo, pltpu.roll(hi, HALF, 1)).astype(jnp.bfloat16)
            out_ref[HALF:BLOCK, columns] = jnp.where(low_lanes, pltpu.roll(lo, HALF, 1), hi).astype(jnp.bfloat16)
        return 0

    lax.fori_loop(0, NZ, unpack, 0)

    for t in range(4):
        wait(kv[t % 3].at[pl.ds(0, NY * NZ - 1)], a_send.at[t])
    for i in range(3):
        wait(kbuf.at[pl.ds(0, 2 * NZ * NY)], x_send.at[i])
    wait(kbuf, c_send)
    wait(lists_v.at[0], l_send)

    @pl.when(z_lo != c)
    def _():
        wait(lists_v.at[0], l_send)

    for half in range(2):
        wait(mixed.at[half, pl.ds(0, NY * NZ - 1)], o_send.at[half])


def on_device(query_rows, key_rows, value_rows, block_lists):
    dma = pltpu.SemaphoreType.DMA
    return pl.pallas_call(
        kernel,
        out_shape=jax.ShapeDtypeStruct(query_rows.shape, jnp.bfloat16),
        in_specs=[pl.BlockSpec(memory_space=pl.ANY)] * 4,
        out_specs=pl.BlockSpec(memory_space=pltpu.VMEM),
        scratch_shapes=[
            pltpu.VMEM((2 * SLABS, BLOCK, BLOCK), jnp.bfloat16),
            pltpu.VMEM((2 * SLABS, HALF, BLOCK), jnp.bfloat16),
            pltpu.VMEM((2 * SLABS, HALF, BLOCK), jnp.bfloat16),
            pltpu.VMEM((NY * NZ, BLOCK, BLOCK), jnp.bfloat16),
            pltpu.VMEM(value_rows.shape, jnp.bfloat16),
            pltpu.VMEM((NY * NZ, HALF, BLOCK), jnp.bfloat16),
            pltpu.VMEM((NY * NZ, HALF, BLOCK), jnp.bfloat16),
            pltpu.VMEM((NY * NZ, 2 * BLOCK, LIVE * HALF), jnp.bfloat16),
            pltpu.VMEM((NY * NZ, HALF, BLOCK), jnp.float32),
            pltpu.VMEM((2, NY * NZ, HALF, BLOCK), jnp.bfloat16),
            pltpu.VMEM((2, NY * NZ, HALF, BLOCK), jnp.bfloat16),
            pltpu.VMEM((2, LIVE, 32), jnp.int32),
            pltpu.VMEM((2, LIVE, 32), jnp.int32),
            pltpu.SMEM((2, LIVE, 32), jnp.int32),
            dma, dma((4,)), dma((NY,)), dma((4, NZ)), dma((3,)), dma((3, NZ)), dma((3, NZ)), dma((3, NZ)), dma, dma((3,)),
            dma, dma, dma, dma((2,)), dma((2, NZ)),
        ],
        compiler_params=pltpu.CompilerParams(collective_id=0, has_side_effects=True, vmem_limit_bytes=52 * 2**20),
        name="attention",
    )(query_rows, key_rows, value_rows, jnp.swapaxes(block_lists, 1, 2))


def solution(mesh):
    in_specs = (P(("blk", "head"), None), P(("blk", "head"), None), P(("blk", "head"), None), P("head", "blk", None))
    return jax.shard_map(
        on_device, mesh=mesh, in_specs=in_specs, out_specs=P(("blk", "head"), None), check_vma=False
    )
```
